512 devices in a mesh: inner: 32 (over y, x), outer: 16 (over z, core).
Axes of the slice: x: 4, y: 8, z: 8, core: 2. Of those that a mesh axis runs over, the one named last changes fastest.
Arguments:
- query: bfloat16 [65536, 768], P(('inner', 'outer')), may hold values from -8 to 8
- keys: bfloat16 [65536, 768], P(('inner', 'outer')), may hold values from -8 to 8
- values: bfloat16 [65536, 768], P(('inner', 'outer')), may hold values from -6 to 6
- dout: bfloat16 [65536, 768], P(('inner', 'outer')), may hold values from -6 to 6
- partners: int32 [512, 7], P(('inner', 'outer')), may hold values from 0 to 511, as said below
- counts: int32 [512], P(('inner', 'outer')), may hold values from 1 to 7, as said below
Outputs:
- dquery: bfloat16 [65536, 768], P(('inner', 'outer'))
- dkeys: bfloat16 [65536, 768], P(('inner', 'outer'))
- dvalues: bfloat16 [65536, 768], P(('inner', 'outer'))
The draws below stay inside these ranges and needn't reach their ends.
Inputs may be any that keep to these rules, and one draw needn't show every extreme that they name: Block b has the coordinates z = b mod 16, x = (b div 16) mod 4, y = b div (64). partners[b, 0] is b; slots 1 to counts[b] - 1 hold distinct blocks that differ from b by one step in exactly one of x, y, z and lie in the volume (x below 4, y below 8, z below 16), in the order x+1, x-1, y+1, y-1, z+1, z-1 of those present; the remaining slots hold b. counts[b] is one more than the number of neighbours that block b lists; some block lists every neighbour it has in the volume.
All inputs are finite; a program needn't handle non-finite values.
Results may differ from the reference program's by a relative error of at most 0.011.
Values may be sent and summed in bfloat16 or wider, within the bound.
No kernel may reach another device: no remote copies, remote signals or barrier semaphores. Data moves between devices by JAX's collectives and lax.ppermute only.
A program may use at most 64 MiB of HBM per device.

```python
from functools import reduce
import jax
import jax.numpy as jnp
from jax import lax

HEADS = 6
HD = 128
BLOCK = 128
ROW_W = 4
MAXP = 7
BLOCKS = 512
TOKENS = 65536
N_INNER = 32
N_OUTER = 16


def neighbour_table(key):
    block_ids = jnp.arange(BLOCKS, dtype=jnp.int32)
    zpos = block_ids % N_OUTER
    inner_pos = block_ids // N_OUTER
    xpos = inner_pos % ROW_W
    ypos = inner_pos // ROW_W
    rows_y = N_INNER // ROW_W
    valid = jnp.stack([xpos < ROW_W - 1, xpos > 0, ypos < rows_y - 1, ypos > 0, zpos < N_OUTER - 1, zpos > 0], axis=1)
    key_level, key_pick, key_y, key_z = jax.random.split(key, 4)
    level = jax.random.randint(key_level, (BLOCKS, 1), 2, 8)
    picked = jax.random.randint(key_pick, (BLOCKS, 6), 0, 8) < level
    full_y = jax.random.randint(key_y, (), 1, max(rows_y - 1, 2))
    full_z = jax.random.randint(key_z, (), 1, max(N_OUTER - 1, 2))
    full_id = (full_y * ROW_W + 1) * N_OUTER + full_z
    chosen = valid & (picked | (block_ids == full_id)[:, None])
    offsets = jnp.array([N_OUTER, -N_OUTER, ROW_W * N_OUTER, -ROW_W * N_OUTER, 1, -1], jnp.int32)
    neighbours = block_ids[:, None] + offsets[None, :]
    slot = jnp.cumsum(chosen.astype(jnp.int32), axis=1)
    table = jnp.broadcast_to(block_ids[:, None], (BLOCKS, MAXP))
    for column in range(6):
        target = jnp.where(chosen[:, column], slot[:, column], 0)
        table = table.at[block_ids, target].set(jnp.where(chosen[:, column], neighbours[:, column], block_ids))
    return (table.astype(jnp.int32), (1 + slot[:, 5]).astype(jnp.int32))


def draw_partners(key, part):
    table, listed = neighbour_table(key)
    return table


def draw_counts(key, part):
    table, listed = neighbour_table(key)
    return listed


def draw_query(key, part):
    key = jax.random.fold_in(key, 11)
    shape = (BLOCKS, BLOCK, HEADS * HD)
    base = jnp.clip(jax.random.normal(key, shape, jnp.float32), -6.0, 6.0)
    return base.reshape(TOKENS, HEADS * HD).astype(jnp.bfloat16)


def draw_keys(key, part):
    key = jax.random.fold_in(key, 12)
    shape = (BLOCKS, BLOCK, HEADS * HD)
    base = jnp.clip(jax.random.normal(key, shape, jnp.float32), -6.0, 6.0)
    return base.reshape(TOKENS, HEADS * HD).astype(jnp.bfloat16)


def block_levels(key, dims, cuts, smallest, high):
    loudness, own = 1.0, jax.random.fold_in(key, 6)
    for position, parts in cuts:
        draws = jnp.exp(jax.random.uniform(jax.random.fold_in(own, position), (parts,), jnp.float32, smallest / len(cuts), high / len(cuts)))
        loudness = loudness * jnp.repeat(draws, dims[position] // parts).reshape([-1 if axis == position else 1 for axis in range(len(dims))])
    return loudness


def normal_values(own_key, dims, scale, bound, cuts=(), kind=jnp.bfloat16):
    values = jax.random.normal(own_key, dims, jnp.float32) * scale
    if len(cuts) > 0:
        values = block_levels(own_key, dims, cuts, -0.22, 0.18) * values
    return jnp.clip(values, min=-bound, max=bound).astype(kind)


def setup_inputs(seed: int = 0) -> dict:
    splits = jax.random.split(jax.random.key(seed), 7)
    return {
        "query": draw_query(jax.random.fold_in(splits[6], 71), 0),
        "keys": draw_keys(jax.random.fold_in(splits[6], 71), 0),
        "values": normal_values(splits[2], (TOKENS, HEADS * HD), 1.0, 6.0, ((0, 512),)),
        "dout": normal_values(splits[3], (TOKENS, HEADS * HD), 1.0, 6.0, ((0, 512),)),
        "partners": draw_partners(jax.random.fold_in(splits[6], 71), 0),
        "counts": draw_counts(jax.random.fold_in(splits[6], 71), 0),
    }


neg_large = -1.0e30


def offset_list():
    return [N_OUTER, -N_OUTER, ROW_W * N_OUTER, -ROW_W * N_OUTER, 1, -1]


def take_block(matrix, block):
    start = (jnp.clip(block, 0, BLOCKS - 1) * BLOCK).astype(jnp.int32)
    piece = lax.dynamic_slice_in_dim(matrix, start, BLOCK, 0)
    return piece.reshape(BLOCK, HEADS, HD).astype(jnp.float32)


def rounded(matrix):
    return lax.optimization_barrier(matrix.astype(jnp.bfloat16)).astype(jnp.float32)


def scores_of(query_heads, key_heads):
    return jnp.einsum("qhd,khd->hqk", query_heads, key_heads) * HD ** -0.5


def pair_flags(partners, counts):
    block_ids = jnp.arange(BLOCKS, dtype=jnp.int32)
    live_slots = jnp.arange(MAXP, dtype=jnp.int32)[None, :] < counts[:, None]
    columns = [jnp.any((partners == (block_ids + step)[:, None]) & live_slots, axis=1) for step in offset_list()]
    return jnp.stack(columns, axis=1)


def reference(query, keys, values, dout, partners, counts):
    scale = HD ** -0.5
    flags = pair_flags(partners, counts)
    steps = offset_list()

    def query_pass(block):
        query_heads = take_block(query, block)
        dout_heads = take_block(dout, block)
        sources = [block] + [block + step for step in steps]
        score_list = []
        for index in range(len(sources)):
            scores = scores_of(query_heads, take_block(keys, sources[index]))
            if index > 0:
                scores = jnp.where(flags[block, index - 1], scores, neg_large)
            score_list.append(scores)
        row_max = reduce(jnp.maximum, [scores.max(axis=2) for scores in score_list])
        total = sum(jnp.sum(jnp.exp(scores - row_max[:, :, None]), axis=2) for scores in score_list)
        log_total = row_max + jnp.log(total)
        probs = [jnp.exp(scores - log_total[:, :, None]) for scores in score_list]
        attended = jnp.zeros((BLOCK, HEADS, HD), jnp.float32)
        for index in range(len(sources)):
            attended = attended + jnp.einsum("hqk,khd->qhd", rounded(probs[index]), take_block(values, sources[index]))
        delta = jnp.sum(dout_heads * attended, axis=2).T
        query_grad = jnp.zeros((BLOCK, HEADS, HD), jnp.float32)
        for index in range(len(sources)):
            value_heads = take_block(values, sources[index])
            dprobs = jnp.einsum("qhd,khd->hqk", dout_heads, value_heads)
            dscores = rounded(probs[index] * (dprobs - delta[:, :, None]))
            query_grad = query_grad + jnp.einsum("hqk,khd->qhd", dscores, take_block(keys, sources[index]))
        query_grad = (query_grad * scale).astype(jnp.bfloat16).reshape(BLOCK, HEADS * HD)
        return query_grad, log_total, delta

    block_ids = jnp.arange(BLOCKS, dtype=jnp.int32)
    query_grads, totals, deltas = lax.map(query_pass, block_ids)

    def key_pass(block):
        key_heads = take_block(keys, block)
        value_heads = take_block(values, block)
        key_grad = jnp.zeros((BLOCK, HEADS, HD), jnp.float32)
        value_grad = jnp.zeros((BLOCK, HEADS, HD), jnp.float32)
        sources = [(block, jnp.array(True))]
        for column in range(len(steps)):
            source = block - steps[column]
            clipped = jnp.clip(source, 0, BLOCKS - 1).astype(jnp.int32)
            live = (source >= 0) & (source < BLOCKS) & flags[clipped, column]
            sources.append((source, live))
        for source, live in sources:
            clipped = jnp.clip(source, 0, BLOCKS - 1).astype(jnp.int32)
            query_heads = take_block(query, clipped)
            dout_heads = take_block(dout, clipped)
            scores = scores_of(query_heads, key_heads)
            probs = jnp.where(live, jnp.exp(scores - totals[clipped][:, :, None]), 0.0)
            dprobs = jnp.einsum("qhd,khd->hqk", dout_heads, value_heads)
            dscores = rounded(probs * (dprobs - deltas[clipped][:, :, None]))
            key_grad = key_grad + jnp.einsum("hqk,qhd->khd", dscores, query_heads)
            value_grad = value_grad + jnp.einsum("hqk,qhd->khd", rounded(probs), dout_heads)
        key_grad = (key_grad * scale).astype(jnp.bfloat16).reshape(BLOCK, HEADS * HD)
        value_grad = value_grad.astype(jnp.bfloat16).reshape(BLOCK, HEADS * HD)
        return key_grad, value_grad

    key_grads, value_grads = lax.map(key_pass, block_ids)
    width = HEADS * HD
    return (query_grads.reshape(TOKENS, width), key_grads.reshape(TOKENS, width), value_grads.reshape(TOKENS, width))
```

```python
import functools

import jax
import jax.numpy as jnp
from jax import lax
from jax.experimental import pallas as pl
from jax.experimental.pallas import tpu as pltpu
from jax.sharding import PartitionSpec as P

HEADS = 6
HD = 128
BLOCK = 128
NX, NY, NZ = 4, 8, 16
AXES = ("inner", "outer")
SCALE = HD ** -0.5
LOG2E = 1.4426950408889634
NEG = -1e30
X_STEP, Y_STEP, Z_STEP = NZ, NZ * NX, 1
ROUTES = (("y", 1), ("y", -1), ("x", 1), ("x", -1), ("z", 1), ("z", -1))
STEP = {"x": X_STEP, "y": Y_STEP, "z": Z_STEP}
SIZE = {"x": NX, "y": NY, "z": NZ}


def coordinate(block, name):
    return (block // STEP[name]) % SIZE[name]


def pairs(name, direction):
    return [
        (b, b + direction * STEP[name])
        for b in range(NX * NY * NZ)
        if 0 <= coordinate(b, name) + direction < SIZE[name]
    ]


def moved(message, name, direction):
    return lax.ppermute(message, AXES, pairs(name, direction))


def rows_of(ref, half, head):
    return ref[pl.ds(half * BLOCK, BLOCK), pl.ds(head * HD, HD)]


def nt(a, b):
    return lax.dot_general(a, b, (((1,), (1,)), ((), ())), preferred_element_type=jnp.float32)


def nn(a, b):
    return lax.dot_general(a, b, (((1,), (0,)), ((), ())), preferred_element_type=jnp.float32)


def tn(a, b):
    return lax.dot_general(a, b, (((0,), (0,)), ((), ())), preferred_element_type=jnp.float32)


def pair_kernel(partners, counts, query, dout, own, *refs):
    others, outs = refs[:6], refs[6:]
    terms, query_out, own_out = outs[:6], outs[6], outs[7]
    blocks = (own,) + tuple(others)
    me = partners[0, 0]
    biases = [0.0]
    for name, direction in ROUTES:
        target = me - direction * STEP[name]
        listed = jnp.int32(0)
        for slot in range(1, 7):
            hit = (partners[0, slot] == target) & (slot < counts[0])
            listed = listed | hit.astype(jnp.int32)
        biases.append(jnp.where(listed > 0, jnp.float32(0.0), jnp.float32(NEG)))
    for head in range(HEADS):
        lanes = pl.ds(head * HD, HD)
        q = query[:, lanes]
        do = dout[:, lanes]
        scores = [nt(rows_of(block, 0, head), q) for block in blocks]
        tops = [
            jnp.max(s, axis=0, keepdims=True) * (SCALE * LOG2E) + bias
            for s, bias in zip(scores, biases)
        ]
        top = functools.reduce(jnp.maximum, tops)
        weights = [
            jnp.exp2(s * (SCALE * LOG2E) + (bias - top)) for s, bias in zip(scores, biases)
        ]
        grads = [nt(rows_of(block, 1, head), do) for block in blocks]
        total = functools.reduce(
            jnp.add, [jnp.sum(w, axis=0, keepdims=True) for w in weights]
        )
        delta = functools.reduce(
            jnp.add, [jnp.sum(w * g, axis=0, keepdims=True) for w, g in zip(weights, grads)]
        )
        inverse = 1.0 / total
        delta = delta * inverse
        query_grad = jnp.zeros((BLOCK, HD), jnp.float32)
        for index in range(7):
            probs = weights[index] * inverse
            dscores = (probs * (grads[index] - delta)).astype(jnp.bfloat16)
            query_grad = query_grad + tn(dscores, rows_of(blocks[index], 0, head))
            key_grad = nn(dscores, q) * SCALE
            value_grad = nn(probs.astype(jnp.bfloat16), do)
            out = own_out if index == 0 else terms[index - 1]
            out[pl.ds(0, BLOCK), lanes] = key_grad.astype(out.dtype)
            out[pl.ds(BLOCK, BLOCK), lanes] = value_grad.astype(out.dtype)
        query_out[:, lanes] = (query_grad * SCALE).astype(query_out.dtype)


def sum_kernel(own, *refs):
    parts, (key_out, value_out) = refs[:6], refs[6:]
    for half, out in ((0, key_out), (1, value_out)):
        rows = pl.ds(half * BLOCK, BLOCK)
        total = own[rows, :]
        for part in parts:
            total = total + part[rows, :].astype(jnp.float32)
        out[...] = total.astype(out.dtype)


VM = pl.BlockSpec(memory_space=pltpu.VMEM)
SM = pl.BlockSpec(memory_space=pltpu.SMEM)
WIDE = (2 * BLOCK, HEADS * HD)
NARROW = (BLOCK, HEADS * HD)


def on_device(query, keys, values, dout, partners, counts):
    own = jnp.concatenate([keys, values], axis=0)
    others = [moved(own, name, direction) for name, direction in ROUTES]
    outs = pl.pallas_call(
        pair_kernel,
        out_shape=[jax.ShapeDtypeStruct(WIDE, jnp.bfloat16)] * 6
        + [jax.ShapeDtypeStruct(NARROW, jnp.bfloat16), jax.ShapeDtypeStruct(WIDE, jnp.float32)],
        in_specs=[SM, SM] + [VM] * 9,
        out_specs=[VM] * 8,
        compiler_params=pltpu.CompilerParams(vmem_limit_bytes=40 * 1024 * 1024),
        name="pairs",
    )(partners, counts, query, dout, own, *others)
    terms, query_out, own_out = outs[:6], outs[6], outs[7]
    arrived = [
        moved(term, name, -direction) for term, (name, direction) in zip(terms, ROUTES)
    ]
    key_out, value_out = pl.pallas_call(
        sum_kernel,
        out_shape=[jax.ShapeDtypeStruct(NARROW, jnp.bfloat16)] * 2,
        in_specs=[VM] * 7,
        out_specs=[VM] * 2,
        compiler_params=pltpu.CompilerParams(vmem_limit_bytes=40 * 1024 * 1024),
        name="sums",
    )(own_out, *arrived)
    return query_out, key_out, value_out


def solution(mesh):
    tokens = P(AXES, None)
    return jax.shard_map(
        on_device,
        mesh=mesh,
        in_specs=(tokens, tokens, tokens, tokens, tokens, P(AXES)),
        out_specs=(tokens, tokens, tokens),
        check_vma=False,
    )
```

```python
import functools

import jax
import jax.numpy as jnp
from jax import lax
from jax.experimental import pallas as pl
from jax.experimental.pallas import tpu as pltpu
from jax.sharding import PartitionSpec as P

HEADS = 6
HD = 128
BLOCK = 128
AXES = ("inner", "outer")
SCALE = HD ** -0.5
SCALE2 = SCALE * 1.4426950408889634
NEG = -1e30
STEP = {"x": 16, "y": 64, "z": 1}
SIZE = {"x": 4, "y": 8, "z": 16}
BLOCKS = 512
ROUTES = (
    (("z", 1), ("z", 1)),
    (("y", 0), ("x", 0)),
    (("y", 1), ("x", 1)),
    (("x", 0), ("y", 0)),
    (("x", 1), ("y", 1)),
    (("z", 0), ("z", 0)),
)
EARLY = 4
BACK = (0, 1, 2, 3, 4, 5)
SUMMED = 4


def route_pairs(route):
    found = []
    for block in range(BLOCKS):
        name, odd = route[block & 1]
        place = (block // STEP[name]) % SIZE[name]
        sign = 1 - 2 * ((place + odd) & 1)
        if 0 <= place + sign < SIZE[name]:
            found.append((block, block + sign * STEP[name]))
    return found


def swapped(message, index):
    return lax.ppermute(message, AXES, route_pairs(ROUTES[index]))


def partner_of(me, index):
    targets = []
    for name, odd in ROUTES[index]:
        place = lax.div(me, jnp.int32(STEP[name])) & (SIZE[name] - 1)
        sign = 1 - 2 * ((place + odd) & 1)
        targets.append(me + sign * STEP[name])
    return jnp.where((me & 1) == 0, targets[0], targets[1])


def bias_of(partners, me, index):
    target = partner_of(me, index)
    listed = jnp.int32(0)
    for slot in range(1, 7):
        listed = listed | (partners[0, slot] == target).astype(jnp.int32)
    return jnp.where(listed > 0, jnp.float32(0.0), jnp.float32(NEG))


def dot(a, b, da, db):
    return lax.dot_general(a, b, (((da,), (db,)), ((), ())), preferred_element_type=jnp.float32)


KEYS = pl.ds(0, BLOCK)
VALUES = pl.ds(BLOCK, BLOCK)


def lanes_of(head):
    return pl.ds(head * HD, HD)


def score(blocks, q, lanes):
    return [dot(block[KEYS, lanes], q, 1, 1) for block in blocks]


def weigh(scores, blocks, biases, do, lanes, before=None):
    tops = [
        jnp.max(s, axis=0, keepdims=True) * SCALE2 + bias for s, bias in zip(scores, biases)
    ]
    top = functools.reduce(jnp.maximum, tops + ([before] if before is not None else []))
    weights = [jnp.exp2(s * SCALE2 + (bias - top)) for s, bias in zip(scores, biases)]
    grads = [dot(block[VALUES, lanes], do, 1, 1) for block in blocks]
    total = functools.reduce(jnp.add, [jnp.sum(w, axis=0, keepdims=True) for w in weights])
    delta = functools.reduce(
        jnp.add, [jnp.sum(w * g, axis=0, keepdims=True) for w, g in zip(weights, grads)]
    )
    return weights, grads, top, total, delta


def pack_kernel(query, keys, values, dout, own, asks, sems):
    copies = [
        pltpu.make_async_copy(source, target, sems.at[i])
        for i, (source, target) in enumerate(
            (
                (keys, own.at[KEYS, :]),
                (values, own.at[VALUES, :]),
                (query, asks.at[KEYS, :]),
                (dout, asks.at[VALUES, :]),
            )
        )
    ]
    for copy in copies:
        copy.start()
    for copy in copies:
        copy.wait()


def early_kernel(partners, asks, own, *refs):
    blocks, refs = (own,) + refs[:EARLY][::-1], refs[EARLY:]
    weights_out, grads_out, stats_out, partner_list, sem = refs
    fetch = pltpu.make_async_copy(partners, partner_list, sem)
    fetch.start()

    def read_lists():
        fetch.wait()
        me = partner_list[0, 0]
        return [
            jnp.full((1, HD), bias_of(partner_list, me, index), jnp.float32)
            for index in range(6)
        ]

    rows = None
    for head in range(HEADS):
        lanes = lanes_of(head)
        q, do = asks[KEYS, lanes], asks[VALUES, lanes]
        scores = score(blocks, q, lanes)
        if rows is None:
            rows = [jnp.zeros((1, HD), jnp.float32)] + read_lists()
        weights, grads, top, total, delta = weigh(scores, blocks, rows[: EARLY + 1], do, lanes)
        for index in range(EARLY + 1):
            weights_out[index, :, lanes] = weights[index]
            grads_out[index, :, lanes] = grads[index]
        stats_out[0:1, lanes] = top
        stats_out[1:2, lanes] = total
        stats_out[2:3, lanes] = delta
        for index in range(EARLY, 6):
            stats_out[3 + index - EARLY : 4 + index - EARLY, lanes] = rows[1 + index]


def late_kernel(asks, early_weights, early_grads, stats, *refs):
    late = 6 - EARLY
    blocks, refs = refs[:late][::-1], refs[late:]
    terms, dscores_out, final_out = refs[:6], refs[6], refs[7]
    for head in range(HEADS):
        lanes = lanes_of(head)
        q, do = asks[KEYS, lanes], asks[VALUES, lanes]
        before = stats[0:1, lanes]
        rows = [stats[3 + i : 4 + i, lanes] for i in range(late)]
        scores = score(blocks, q, lanes)
        weights, grads, top, total, delta = weigh(scores, blocks, rows, do, lanes, before)
        old = jnp.exp2(before - top)
        total = total + stats[1:2, lanes] * old
        delta = delta + stats[2:3, lanes] * old
        new = 1.0 / total
        delta = delta * new
        old = old * new
        final_out[0:1, lanes] = old
        final_out[1:2, lanes] = delta
        for index in range(6):
            if index < EARLY:
                probs = early_weights[index + 1, :, lanes] * old
                grad = early_grads[index + 1, :, lanes]
            else:
                probs = weights[index - EARLY] * new
                grad = grads[index - EARLY]
            dscores = (probs * (grad - delta)).astype(jnp.bfloat16)
            probs = probs.astype(jnp.bfloat16)
            dscores_out[index, :, lanes] = dscores
            out = terms[index]
            out[KEYS, lanes] = dot(dscores, q, 1, 0).astype(out.dtype)
            out[VALUES, lanes] = dot(probs, do, 1, 0).astype(out.dtype)


def own_kernel(asks, early_weights, early_grads, final, dscores, own, *refs):
    blocks, parts, (query_out, own_out) = refs[:6], refs[6 : 6 + SUMMED], refs[6 + SUMMED :]
    for head in range(HEADS):
        lanes = lanes_of(head)
        probs = early_weights[0, :, lanes] * final[0:1, lanes]
        mine = (probs * (early_grads[0, :, lanes] - final[1:2, lanes])).astype(jnp.bfloat16)
        probs = probs.astype(jnp.bfloat16)
        grad = dot(mine, own[KEYS, lanes], 0, 0)
        for index in range(6):
            grad = grad + dot(dscores[index, :, lanes], blocks[index][KEYS, lanes], 0, 0)
        query_out[:, lanes] = (grad * SCALE).astype(query_out.dtype)
        for rows, low in ((KEYS, mine), (VALUES, probs)):
            total = dot(low, asks[rows, lanes], 1, 0)
            for part in parts:
                total = total + part[rows, lanes].astype(jnp.float32)
            own_out[rows, lanes] = total


def sum_kernel(own, *refs):
    parts, (key_out, value_out) = refs[:-2], refs[-2:]
    for rows, out, scale in ((KEYS, key_out, SCALE), (VALUES, value_out, 1.0)):
        total = own[rows, :]
        for part in parts:
            total = total + part[rows, :].astype(jnp.float32)
        out[...] = (total * scale).astype(out.dtype)


FAR = pl.BlockSpec(memory_space=pltpu.HBM)
VM = pl.BlockSpec(memory_space=pltpu.VMEM)
SM = pl.BlockSpec(memory_space=pltpu.SMEM)
WIDE = (2 * BLOCK, HEADS * HD)
NARROW = (BLOCK, HEADS * HD)


NEAR = pltpu.VMEM
PLAIN = jax.ShapeDtypeStruct


def far(array):
    return pltpu.with_memory_space_constraint(array, pltpu.HBM)


def call(kernel, ins, outs, name, scratch=()):
    return pl.pallas_call(
        kernel,
        out_shape=[
            place(shape, dtype) for place, shape, dtype in outs
        ],
        in_specs=ins,
        out_specs=[VM] * len(outs),
        scratch_shapes=list(scratch),
        compiler_params=pltpu.CompilerParams(vmem_limit_bytes=40 * 1024 * 1024),
        name=name,
    )


def on_device(query, keys, values, dout, partners, counts):
    low, full = jnp.bfloat16, jnp.float32
    own, asks = call(
        pack_kernel,
        [FAR] * 4,
        [(NEAR, WIDE, low)] * 2,
        "pack",
        [pltpu.SemaphoreType.DMA((4,))],
    )(far(query), far(keys), far(values), far(dout))
    blocks = [swapped(own, index) for index in range(6)]
    weights, grads, stats = call(
        early_kernel,
        [FAR] + [VM] * (2 + EARLY),
        [(NEAR, (EARLY + 1,) + NARROW, full)] * 2 + [(NEAR, (8, HEADS * HD), full)],
        "early",
        [
            pltpu.SMEM((1, 7), jnp.int32),
            pltpu.SemaphoreType.DMA,
        ],
    )(far(partners), asks, own, *blocks[:EARLY][::-1])
    outs = call(
        late_kernel,
        [VM] * (4 + 6 - EARLY),
        [(NEAR, WIDE, low)] * 6 + [(NEAR, (6,) + NARROW, low), (NEAR, (8, HEADS * HD), full)],
        "late",
    )(asks, weights, grads, stats, *blocks[EARLY:][::-1])
    terms, dscores, final = outs[:6], outs[6], outs[7]
    arrived = [swapped(terms[index], index) for index in BACK]
    query_out, own_out = call(
        own_kernel, [VM] * (12 + SUMMED), [(PLAIN, NARROW, low), (NEAR, WIDE, full)], "own"
    )(asks, weights, grads, final, dscores, own, *blocks, *arrived[:SUMMED])
    key_out, value_out = call(sum_kernel, [VM] * (7 - SUMMED), [(PLAIN, NARROW, low)] * 2, "sums")(
        own_out, *arrived[SUMMED:]
    )
    return query_out, key_out, value_out


def solution(mesh):
    tokens = P(AXES, None)
    return jax.shard_map(
        on_device,
        mesh=mesh,
        in_specs=(tokens, tokens, tokens, tokens, tokens, P(AXES)),
        out_specs=(tokens, tokens, tokens),
        check_vma=False,
    )
```

```python
import functools

import jax
import jax.numpy as jnp
from jax import lax
from jax.experimental import pallas as pl
from jax.experimental.pallas import tpu as pltpu
from jax.sharding import PartitionSpec as P

HEADS = 6
HD = 128
BLOCK = 128
AXES = ("inner", "outer")
SCALE = HD ** -0.5
SCALE2 = SCALE * 1.4426950408889634
NEG = -1e30
STEP = {"x": 16, "y": 64, "z": 1}
SIZE = {"x": 4, "y": 8, "z": 16}
BLOCKS = 512
ROUTES = (
    (("z", 1), ("z", 1)),
    (("y", 0), ("x", 0)),
    (("y", 1), ("x", 1)),
    (("x", 0), ("y", 0)),
    (("x", 1), ("y", 1)),
    (("z", 0), ("z", 0)),
)
GROUPS = ((0, 1, 2, 3, 4, 5),)
EARLY = 4
BACK = (0, 1, 2, 3, 4, 5)
SUMMED = 4


def route_pairs(route):
    found = []
    for block in range(BLOCKS):
        name, odd = route[block & 1]
        place = (block // STEP[name]) % SIZE[name]
        sign = 1 - 2 * ((place + odd) & 1)
        if 0 <= place + sign < SIZE[name]:
            found.append((block, block + sign * STEP[name]))
    return found


def swapped(message, index):
    return lax.ppermute(message, AXES, route_pairs(ROUTES[index]))


def partner_of(me, index):
    targets = []
    for name, odd in ROUTES[index]:
        place = lax.div(me, jnp.int32(STEP[name])) & (SIZE[name] - 1)
        sign = 1 - 2 * ((place + odd) & 1)
        targets.append(me + sign * STEP[name])
    return jnp.where((me & 1) == 0, targets[0], targets[1])


def bias_of(partners, me, index):
    target = partner_of(me, index)
    listed = jnp.int32(0)
    for slot in range(1, 7):
        listed = listed | (partners[0, slot] == target).astype(jnp.int32)
    return jnp.where(listed > 0, jnp.float32(0.0), jnp.float32(NEG))


def dot(a, b, da, db):
    return lax.dot_general(a, b, (((da,), (db,)), ((), ())), preferred_element_type=jnp.float32)


KEYS = pl.ds(0, BLOCK)
VALUES = pl.ds(BLOCK, BLOCK)


def lanes_of(head):
    return pl.ds(head * HD, HD)


def summed(items):
    return functools.reduce(jnp.add, items)


def weigh(blocks, biases, asks, heads, before=None):
    span = [lanes_of(head) for head in heads]
    scores = [[dot(block[KEYS, l], asks[KEYS, l], 1, 1) for block in blocks] for l in span]
    grads = [[dot(block[VALUES, l], asks[VALUES, l], 1, 1) for block in blocks] for l in span]
    tops = [
        functools.reduce(
            jnp.maximum,
            [
                jnp.max(s, axis=0, keepdims=True) * SCALE2 + bias[:, l]
                for s, bias in zip(row, biases)
            ]
            + ([before[:, l]] if before is not None else []),
        )
        for row, l in zip(scores, span)
    ]
    weights = [
        [jnp.exp2(s * SCALE2 + (bias[:, l] - top)) for s, bias in zip(row, biases)]
        for row, top, l in zip(scores, tops, span)
    ]
    totals = [summed([jnp.sum(w, axis=0, keepdims=True) for w in row]) for row in weights]
    deltas = [
        summed([jnp.sum(w * g, axis=0, keepdims=True) for w, g in zip(row, more)])
        for row, more in zip(weights, grads)
    ]
    return weights, grads, tops, totals, deltas


def pack_kernel(partners, query, keys, values, dout, own, asks, bias_out, partner_list, sems):
    copies = [
        pltpu.make_async_copy(source, target, sems.at[i])
        for i, (source, target) in enumerate(
            (
                (partners, partner_list),
                (keys, own.at[KEYS, :]),
                (values, own.at[VALUES, :]),
                (query, asks.at[KEYS, :]),
                (dout, asks.at[VALUES, :]),
            )
        )
    ]
    for copy in copies:
        copy.start()
    copies[0].wait()
    me = partner_list[0, 0]
    for index in range(6):
        bias = bias_of(partner_list, me, index)
        bias_out[index : index + 1, :] = jnp.full((1, HEADS * HD), bias, jnp.float32)
    for copy in copies[1:]:
        copy.wait()


def early_kernel(asks, biases, own, *refs):
    blocks, refs = (own,) + refs[:EARLY][::-1], refs[EARLY:]
    weights_out, grads_out, stats_out = refs
    rows = [jnp.zeros((1, HEADS * HD), jnp.float32)]
    rows += [biases[index : index + 1, :] for index in range(EARLY)]
    for heads in GROUPS:
        weights, grads, tops, totals, deltas = weigh(blocks, rows, asks, heads)
        for place, head in enumerate(heads):
            lanes = lanes_of(head)
            for index in range(EARLY + 1):
                weights_out[index, :, lanes] = weights[place][index]
                grads_out[index, :, lanes] = grads[place][index]
            stats_out[0:1, lanes] = tops[place]
            stats_out[1:2, lanes] = totals[place]
            stats_out[2:3, lanes] = deltas[place]


def late_kernel(asks, biases, early_weights, early_grads, stats, *refs):
    late = 6 - EARLY
    blocks, refs = refs[:late][::-1], refs[late:]
    terms, dscores_out, final_out = refs[:6], refs[6], refs[7]
    rows = [biases[index : index + 1, :] for index in range(EARLY, 6)]
    before = stats[0:1, :]
    for heads in GROUPS:
        weights, grads, tops, totals, deltas = weigh(blocks, rows, asks, heads, before)
        spread = []
        for place, head in enumerate(heads):
            lanes = lanes_of(head)
            old = jnp.exp2(before[:, lanes] - tops[place])
            new = 1.0 / (totals[place] + stats[1:2, lanes] * old)
            delta = (deltas[place] + stats[2:3, lanes] * old) * new
            final_out[0:1, lanes] = old * new
            final_out[1:2, lanes] = delta
            spread.append((old * new, new, delta))
        for index in range(6):
            for place, head in enumerate(heads):
                lanes = lanes_of(head)
                old, new, delta = spread[place]
                if index < EARLY:
                    probs = early_weights[index + 1, :, lanes] * old
                    grad = early_grads[index + 1, :, lanes]
                else:
                    probs = weights[place][index - EARLY] * new
                    grad = grads[place][index - EARLY]
                dscores = (probs * (grad - delta)).astype(jnp.bfloat16)
                probs = probs.astype(jnp.bfloat16)
                dscores_out[index, :, lanes] = dscores
                out = terms[index]
                out[KEYS, lanes] = dot(dscores, asks[KEYS, lanes], 1, 0).astype(out.dtype)
                out[VALUES, lanes] = dot(probs, asks[VALUES, lanes], 1, 0).astype(out.dtype)


def own_kernel(asks, early_weights, early_grads, final, dscores, own, *refs):
    blocks, parts, (query_out, own_out) = refs[:6], refs[6 : 6 + SUMMED], refs[6 + SUMMED :]
    for heads in GROUPS:
        span = [lanes_of(head) for head in heads]
        probs = [early_weights[0, :, l] * final[0:1, l] for l in span]
        mine = [
            (p * (early_grads[0, :, l] - final[1:2, l])).astype(jnp.bfloat16)
            for p, l in zip(probs, span)
        ]
        probs = [p.astype(jnp.bfloat16) for p in probs]
        grads = [dot(m, own[KEYS, l], 0, 0) for m, l in zip(mine, span)]
        for index in range(6):
            grads = [
                grad + dot(dscores[index, :, l], blocks[index][KEYS, l], 0, 0)
                for grad, l in zip(grads, span)
            ]
        for low, rows in ((mine, KEYS), (probs, VALUES)):
            totals = [dot(m, asks[rows, l], 1, 0) for m, l in zip(low, span)]
            for total, l in zip(totals, span):
                own_out[rows, l] = total + summed(
                    [part[rows, l].astype(jnp.float32) for part in parts]
                )
        for grad, l in zip(grads, span):
            query_out[:, l] = (grad * SCALE).astype(query_out.dtype)


def sum_kernel(own, *refs):
    parts, (key_out, value_out) = refs[:-2], refs[-2:]
    for rows, out, scale in ((KEYS, key_out, SCALE), (VALUES, value_out, 1.0)):
        total = own[rows, :]
        for part in parts:
            total = total + part[rows, :].astype(jnp.float32)
        out[...] = (total * scale).astype(out.dtype)


FAR = pl.BlockSpec(memory_space=pltpu.HBM)
VM = pl.BlockSpec(memory_space=pltpu.VMEM)
SM = pl.BlockSpec(memory_space=pltpu.SMEM)
WIDE = (2 * BLOCK, HEADS * HD)
NARROW = (BLOCK, HEADS * HD)


NEAR = pltpu.VMEM
PLAIN = jax.ShapeDtypeStruct


def far(array):
    return pltpu.with_memory_space_constraint(array, pltpu.HBM)


def call(kernel, ins, outs, name, scratch=()):
    return pl.pallas_call(
        kernel,
        out_shape=[
            place(shape, dtype) for place, shape, dtype in outs
        ],
        in_specs=ins,
        out_specs=[VM] * len(outs),
        scratch_shapes=list(scratch),
        compiler_params=pltpu.CompilerParams(vmem_limit_bytes=40 * 1024 * 1024),
        name=name,
    )


def on_device(query, keys, values, dout, partners, counts):
    low, full = jnp.bfloat16, jnp.float32
    stats_row = (NEAR, (8, HEADS * HD), full)
    own, asks, biases = call(
        pack_kernel,
        [FAR] * 5,
        [(NEAR, WIDE, low)] * 2 + [stats_row],
        "pack",
        [pltpu.SMEM((1, 7), jnp.int32), pltpu.SemaphoreType.DMA((5,))],
    )(far(partners), far(query), far(keys), far(values), far(dout))
    blocks = [swapped(own, index) for index in range(6)]
    weights, grads, stats = call(
        early_kernel,
        [VM] * (3 + EARLY),
        [(NEAR, (EARLY + 1,) + NARROW, full)] * 2 + [stats_row],
        "early",
    )(asks, biases, own, *blocks[:EARLY][::-1])
    outs = call(
        late_kernel,
        [VM] * (5 + 6 - EARLY),
        [(NEAR, WIDE, low)] * 6 + [(NEAR, (6,) + NARROW, low), stats_row],
        "late",
    )(asks, biases, weights, grads, stats, *blocks[EARLY:][::-1])
    terms, dscores, final = outs[:6], outs[6], outs[7]
    arrived = [swapped(terms[index], index) for index in BACK]
    query_out, own_out = call(
        own_kernel, [VM] * (12 + SUMMED), [(PLAIN, NARROW, low), (NEAR, WIDE, full)], "own"
    )(asks, weights, grads, final, dscores, own, *blocks, *arrived[:SUMMED])
    key_out, value_out = call(sum_kernel, [VM] * (7 - SUMMED), [(PLAIN, NARROW, low)] * 2, "sums")(
        own_out, *arrived[SUMMED:]
    )
    return query_out, key_out, value_out


def solution(mesh):
    tokens = P(AXES, None)
    return jax.shard_map(
        on_device,
        mesh=mesh,
        in_specs=(tokens, tokens, tokens, tokens, tokens, P(AXES)),
        out_specs=(tokens, tokens, tokens),
        check_vma=False,
    )
```

```python
import functools

import jax
import jax.numpy as jnp
from jax import lax
from jax.experimental import pallas as pl
from jax.experimental.pallas import tpu as pltpu
from jax.sharding import PartitionSpec as P

HEADS = 6
HD = 128
BLOCK = 128
AXES = ("inner", "outer")
SCALE = HD ** -0.5
SCALE2 = SCALE * 1.4426950408889634
NEG = -1e30
STEP = {"x": 16, "y": 64, "z": 1}
SIZE = {"x": 4, "y": 8, "z": 16}
BLOCKS = 512
ROUTES = (
    (("z", 1), ("z", 1)),
    (("y", 0), ("x", 0)),
    (("y", 1), ("x", 1)),
    (("x", 0), ("y", 0)),
    (("x", 1), ("y", 1)),
    (("z", 0), ("z", 0)),
)
GROUPS = ((0, 1, 2, 3, 4, 5),)
EARLY = 4
BACK = (0, 1, 2, 3, 4, 5)
SUMMED = 3


def route_pairs(route):
    found = []
    for block in range(BLOCKS):
        name, odd = route[block & 1]
        place = (block // STEP[name]) % SIZE[name]
        sign = 1 - 2 * ((place + odd) & 1)
        if 0 <= place + sign < SIZE[name]:
            found.append((block, block + sign * STEP[name]))
    return found


def swapped(message, index):
    return lax.ppermute(message, AXES, route_pairs(ROUTES[index]))


def partner_of(me, index):
    targets = []
    for name, odd in ROUTES[index]:
        place = lax.div(me, jnp.int32(STEP[name])) & (SIZE[name] - 1)
        sign = 1 - 2 * ((place + odd) & 1)
        targets.append(me + sign * STEP[name])
    return jnp.where((me & 1) == 0, targets[0], targets[1])


def bias_of(partners, me, index):
    target = partner_of(me, index)
    listed = jnp.int32(0)
    for slot in range(1, 7):
        listed = listed | (partners[0, slot] == target).astype(jnp.int32)
    return jnp.where(listed > 0, jnp.float32(0.0), jnp.float32(NEG))


def dot(a, b, da, db):
    return lax.dot_general(a, b, (((da,), (db,)), ((), ())), preferred_element_type=jnp.float32)


KEYS = pl.ds(0, BLOCK)
VALUES = pl.ds(BLOCK, BLOCK)


def lanes_of(head):
    return pl.ds(head * HD, HD)


def summed(items):
    return functools.reduce(jnp.add, items)


def weigh(blocks, biases, asks, heads, before=None):
    span = [lanes_of(head) for head in heads]
    scores = [[dot(block[KEYS, l], asks[KEYS, l], 1, 1) for block in blocks] for l in span]
    grads = [[dot(block[VALUES, l], asks[VALUES, l], 1, 1) for block in blocks] for l in span]
    tops = [
        functools.reduce(
            jnp.maximum,
            [
                jnp.max(s, axis=0, keepdims=True) * SCALE2 + bias[:, l]
                for s, bias in zip(row, biases)
            ]
            + ([before[:, l]] if before is not None else []),
        )
        for row, l in zip(scores, span)
    ]
    weights = [
        [jnp.exp2(s * SCALE2 + (bias[:, l] - top)) for s, bias in zip(row, biases)]
        for row, top, l in zip(scores, tops, span)
    ]
    totals = [summed([jnp.sum(w, axis=0, keepdims=True) for w in row]) for row in weights]
    deltas = [
        summed([jnp.sum(w * g, axis=0, keepdims=True) for w, g in zip(row, more)])
        for row, more in zip(weights, grads)
    ]
    return weights, grads, tops, totals, deltas


def copied(pairs, sems):
    copies = [
        pltpu.make_async_copy(source, target, sems.at[i])
        for i, (source, target) in enumerate(pairs)
    ]
    for copy in copies:
        copy.start()
    return copies


def pack_kernel(keys, values, own, sems):
    for copy in copied(((keys, own.at[KEYS, :]), (values, own.at[VALUES, :])), sems):
        copy.wait()


def load_kernel(partners, query, dout, asks, bias_out, partner_list, sems):
    copies = copied(
        ((partners, partner_list), (query, asks.at[KEYS, :]), (dout, asks.at[VALUES, :])), sems
    )
    copies[0].wait()
    me = partner_list[0, 0]
    for index in range(6):
        bias = bias_of(partner_list, me, index)
        bias_out[index : index + 1, :] = jnp.full((1, HEADS * HD), bias, jnp.float32)
    for copy in copies[1:]:
        copy.wait()


def early_kernel(asks, biases, own, *refs):
    blocks, refs = (own,) + refs[:EARLY][::-1], refs[EARLY:]
    weights_out, grads_out, stats_out = refs
    rows = [jnp.zeros((1, HEADS * HD), jnp.float32)]
    rows += [biases[index : index + 1, :] for index in range(EARLY)]
    for heads in GROUPS:
        weights, grads, tops, totals, deltas = weigh(blocks, rows, asks, heads)
        for place, head in enumerate(heads):
            lanes = lanes_of(head)
            for index in range(EARLY + 1):
                weights_out[index, :, lanes] = weights[place][index]
                grads_out[index, :, lanes] = grads[place][index]
            stats_out[0:1, lanes] = tops[place]
            stats_out[1:2, lanes] = totals[place]
            stats_out[2:3, lanes] = deltas[place]


def late_kernel(asks, biases, early_weights, early_grads, stats, *refs):
    late = 6 - EARLY
    blocks, refs = refs[:late][::-1], refs[late:]
    terms, dscores_out, final_out = refs[:6], refs[6], refs[7]
    rows = [biases[index : index + 1, :] for index in range(EARLY, 6)]
    before = stats[0:1, :]
    for heads in GROUPS:
        weights, grads, tops, totals, deltas = weigh(blocks, rows, asks, heads, before)
        spread = []
        for place, head in enumerate(heads):
            lanes = lanes_of(head)
            old = jnp.exp2(before[:, lanes] - tops[place])
            new = 1.0 / (totals[place] + stats[1:2, lanes] * old)
            delta = (deltas[place] + stats[2:3, lanes] * old) * new
            final_out[0:1, lanes] = old * new
            final_out[1:2, lanes] = delta
            spread.append((old * new, new, delta))
        for index in range(6):
            for place, head in enumerate(heads):
                lanes = lanes_of(head)
                old, new, delta = spread[place]
                if index < EARLY:
                    probs = early_weights[index + 1, :, lanes] * old
                    grad = early_grads[index + 1, :, lanes]
                else:
                    probs = weights[place][index - EARLY] * new
                    grad = grads[place][index - EARLY]
                dscores = (probs * (grad - delta)).astype(jnp.bfloat16)
                probs = probs.astype(jnp.bfloat16)
                dscores_out[index, :, lanes] = dscores
                out = terms[index]
                out[KEYS, lanes] = dot(dscores, asks[KEYS, lanes], 1, 0).astype(out.dtype)
                out[VALUES, lanes] = dot(probs, asks[VALUES, lanes], 1, 0).astype(out.dtype)


def own_kernel(asks, early_weights, early_grads, final, dscores, own, *refs):
    blocks, parts, (query_out, own_out) = refs[:6], refs[6 : 6 + SUMMED], refs[6 + SUMMED :]
    for heads in GROUPS:
        span = [lanes_of(head) for head in heads]
        probs = [early_weights[0, :, l] * final[0:1, l] for l in span]
        mine = [
            (p * (early_grads[0, :, l] - final[1:2, l])).astype(jnp.bfloat16)
            for p, l in zip(probs, span)
        ]
        probs = [p.astype(jnp.bfloat16) for p in probs]
        grads = [dot(m, own[KEYS, l], 0, 0) for m, l in zip(mine, span)]
        for index in range(6):
            grads = [
                grad + dot(dscores[index, :, l], blocks[index][KEYS, l], 0, 0)
                for grad, l in zip(grads, span)
            ]
        for low, rows in ((mine, KEYS), (probs, VALUES)):
            totals = [dot(m, asks[rows, l], 1, 0) for m, l in zip(low, span)]
            for total, l in zip(totals, span):
                own_out[rows, l] = total + summed(
                    [part[rows, l].astype(jnp.float32) for part in parts]
                )
        for grad, l in zip(grads, span):
            query_out[:, l] = (grad * SCALE).astype(query_out.dtype)


def sum_kernel(own, *refs):
    parts, (key_out, value_out) = refs[:-2], refs[-2:]
    for rows, out, scale in ((KEYS, key_out, SCALE), (VALUES, value_out, 1.0)):
        total = own[rows, :]
        for part in parts:
            total = total + part[rows, :].astype(jnp.float32)
        out[...] = (total * scale).astype(out.dtype)


FAR = pl.BlockSpec(memory_space=pltpu.HBM)
VM = pl.BlockSpec(memory_space=pltpu.VMEM)
SM = pl.BlockSpec(memory_space=pltpu.SMEM)
WIDE = (2 * BLOCK, HEADS * HD)
NARROW = (BLOCK, HEADS * HD)


NEAR = pltpu.VMEM
PLAIN = jax.ShapeDtypeStruct


def far(array):
    return pltpu.with_memory_space_constraint(array, pltpu.HBM)


def call(kernel, ins, outs, name, scratch=()):
    return pl.pallas_call(
        kernel,
        out_shape=[
            place(shape, dtype) for place, shape, dtype in outs
        ],
        in_specs=ins,
        out_specs=[VM] * len(outs),
        scratch_shapes=list(scratch),
        compiler_params=pltpu.CompilerParams(vmem_limit_bytes=40 * 1024 * 1024),
        name=name,
    )


def on_device(query, keys, values, dout, partners, counts):
    low, full = jnp.bfloat16, jnp.float32
    stats_row = (NEAR, (8, HEADS * HD), full)
    (own,) = call(
        pack_kernel, [FAR] * 2, [(NEAR, WIDE, low)], "pack", [pltpu.SemaphoreType.DMA((2,))]
    )(far(keys), far(values))
    asks, biases = call(
        load_kernel,
        [FAR] * 3,
        [(NEAR, WIDE, low), stats_row],
        "load",
        [pltpu.SMEM((1, 7), jnp.int32), pltpu.SemaphoreType.DMA((3,))],
    )(far(partners), far(query), far(dout))
    blocks = [swapped(own, index) for index in range(6)]
    weights, grads, stats = call(
        early_kernel,
        [VM] * (3 + EARLY),
        [(NEAR, (EARLY + 1,) + NARROW, full)] * 2 + [stats_row],
        "early",
    )(asks, biases, own, *blocks[:EARLY][::-1])
    outs = call(
        late_kernel,
        [VM] * (5 + 6 - EARLY),
        [(NEAR, WIDE, low)] * 6 + [(NEAR, (6,) + NARROW, low), stats_row],
        "late",
    )(asks, biases, weights, grads, stats, *blocks[EARLY:][::-1])
    terms, dscores, final = outs[:6], outs[6], outs[7]
    arrived = [swapped(terms[index], index) for index in BACK]
    query_out, own_out = call(
        own_kernel, [VM] * (12 + SUMMED), [(PLAIN, NARROW, low), (NEAR, WIDE, full)], "own"
    )(asks, weights, grads, final, dscores, own, *blocks, *arrived[:SUMMED])
    key_out, value_out = call(sum_kernel, [VM] * (7 - SUMMED), [(PLAIN, NARROW, low)] * 2, "sums")(
        own_out, *arrived[SUMMED:]
    )
    return query_out, key_out, value_out


def solution(mesh):
    tokens = P(AXES, None)
    return jax.shard_map(
        on_device,
        mesh=mesh,
        in_specs=(tokens, tokens, tokens, tokens, tokens, P(AXES)),
        out_specs=(tokens, tokens, tokens),
        check_vma=False,
    )
```

```python
import functools

import jax
import jax.numpy as jnp
from jax import lax
from jax.experimental import pallas as pl
from jax.experimental.pallas import tpu as pltpu
from jax.sharding import PartitionSpec as P

HEADS = 6
HD = 128
BLOCK = 128
AXES = ("inner", "outer")
SCALE = HD ** -0.5
SCALE2 = SCALE * 1.4426950408889634
NEG = -1e30
STEP = {"x": 16, "y": 64, "z": 1}
SIZE = {"x": 4, "y": 8, "z": 16}
BLOCKS = 512
ROUTES = (
    (("z", 1), ("z", 1)),
    (("y", 0), ("x", 0)),
    (("y", 1), ("x", 1)),
    (("x", 0), ("y", 0)),
    (("x", 1), ("y", 1)),
    (("z", 0), ("z", 0)),
)
GROUPS = ((0, 1, 2, 3, 4, 5),)
EARLY = 3
BACK = (0, 1, 2, 3, 4, 5)
SUMMED = 3


def route_pairs(route):
    found = []
    for block in range(BLOCKS):
        name, odd = route[block & 1]
        place = (block // STEP[name]) % SIZE[name]
        sign = 1 - 2 * ((place + odd) & 1)
        if 0 <= place + sign < SIZE[name]:
            found.append((block, block + sign * STEP[name]))
    return found


def swapped(message, index):
    return lax.ppermute(message, AXES, route_pairs(ROUTES[index]))


def partner_of(me, index):
    targets = []
    for name, odd in ROUTES[index]:
        place = lax.div(me, jnp.int32(STEP[name])) & (SIZE[name] - 1)
        sign = 1 - 2 * ((place + odd) & 1)
        targets.append(me + sign * STEP[name])
    return jnp.where((me & 1) == 0, targets[0], targets[1])


def bias_of(partners, me, index):
    target = partner_of(me, index)
    listed = jnp.int32(0)
    for slot in range(1, 7):
        listed = listed | (partners[0, slot] == target).astype(jnp.int32)
    return jnp.where(listed > 0, jnp.float32(0.0), jnp.float32(NEG))


def dot(a, b, da, db):
    return lax.dot_general(a, b, (((da,), (db,)), ((), ())), preferred_element_type=jnp.float32)


KEYS = pl.ds(0, BLOCK)
VALUES = pl.ds(BLOCK, BLOCK)


def lanes_of(head):
    return pl.ds(head * HD, HD)


def summed(items):
    return functools.reduce(jnp.add, items)


def weigh(blocks, biases, asks, heads, before=None):
    span = [lanes_of(head) for head in heads]
    scores = [[dot(block[KEYS, l], asks[KEYS, l], 1, 1) for block in blocks] for l in span]
    grads = [[dot(block[VALUES, l], asks[VALUES, l], 1, 1) for block in blocks] for l in span]
    tops = [
        functools.reduce(
            jnp.maximum,
            [
                jnp.max(s, axis=0, keepdims=True) * SCALE2 + bias[:, l]
                for s, bias in zip(row, biases)
            ]
            + ([before[:, l]] if before is not None else []),
        )
        for row, l in zip(scores, span)
    ]
    weights = [
        [jnp.exp2(s * SCALE2 + (bias[:, l] - top)) for s, bias in zip(row, biases)]
        for row, top, l in zip(scores, tops, span)
    ]
    totals = [summed([jnp.sum(w, axis=0, keepdims=True) for w in row]) for row in weights]
    deltas = [
        summed([jnp.sum(w * g, axis=0, keepdims=True) for w, g in zip(row, more)])
        for row, more in zip(weights, grads)
    ]
    return weights, grads, tops, totals, deltas


def copied(pairs, sems):
    copies = [
        pltpu.make_async_copy(source, target, sems.at[i])
        for i, (source, target) in enumerate(pairs)
    ]
    for copy in copies:
        copy.start()
    return copies


def pack_kernel(keys, values, own, sems):
    for copy in copied(((keys, own.at[KEYS, :]), (values, own.at[VALUES, :])), sems):
        copy.wait()


def load_kernel(partners, query, dout, asks, bias_out, partner_list, sems):
    copies = copied(
        ((partners, partner_list), (query, asks.at[KEYS, :]), (dout, asks.at[VALUES, :])), sems
    )
    copies[0].wait()
    me = partner_list[0, 0]
    for index in range(6):
        bias = bias_of(partner_list, me, index)
        bias_out[index : index + 1, :] = jnp.full((1, HEADS * HD), bias, jnp.float32)
    for copy in copies[1:]:
        copy.wait()


def early_kernel(asks, biases, own, *refs):
    blocks, refs = (own,) + refs[:EARLY][::-1], refs[EARLY:]
    weights_out, grads_out, stats_out = refs
    rows = [jnp.zeros((1, HEADS * HD), jnp.float32)]
    rows += [biases[index : index + 1, :] for index in range(EARLY)]
    for heads in GROUPS:
        weights, grads, tops, totals, deltas = weigh(blocks, rows, asks, heads)
        for place, head in enumerate(heads):
            lanes = lanes_of(head)
            for index in range(EARLY + 1):
                weights_out[index, :, lanes] = weights[place][index]
                grads_out[index, :, lanes] = grads[place][index]
            stats_out[0:1, lanes] = tops[place]
            stats_out[1:2, lanes] = totals[place]
            stats_out[2:3, lanes] = deltas[place]


def middle_kernel(asks, biases, stats, block, weights_out, grads_out, stats_out):
    before = stats[0:1, :]
    rows = [biases[EARLY : EARLY + 1, :]]
    for heads in GROUPS:
        weights, grads, tops, totals, deltas = weigh([block], rows, asks, heads, before)
        for place, head in enumerate(heads):
            lanes = lanes_of(head)
            weights_out[:, lanes] = weights[place][0]
            grads_out[:, lanes] = grads[place][0]
            old = jnp.exp2(before[:, lanes] - tops[place])
            stats_out[0:1, lanes] = tops[place]
            stats_out[1:2, lanes] = totals[place] + stats[1:2, lanes] * old
            stats_out[2:3, lanes] = deltas[place] + stats[2:3, lanes] * old


def late_kernel(
    asks, biases, early_weights, early_grads, early_stats, mid_weights, mid_grads, stats, *refs
):
    late = 5 - EARLY
    blocks, refs = refs[:late][::-1], refs[late:]
    terms, dscores_out, final_out = refs[:6], refs[6], refs[7]
    rows = [biases[index : index + 1, :] for index in range(EARLY + 1, 6)]
    before = stats[0:1, :]
    for heads in GROUPS:
        weights, grads, tops, totals, deltas = weigh(blocks, rows, asks, heads, before)
        spread = []
        for place, head in enumerate(heads):
            lanes = lanes_of(head)
            old = jnp.exp2(before[:, lanes] - tops[place])
            new = 1.0 / (totals[place] + stats[1:2, lanes] * old)
            delta = (deltas[place] + stats[2:3, lanes] * old) * new
            first = jnp.exp2(early_stats[0:1, lanes] - tops[place]) * new
            final_out[0:1, lanes] = first
            final_out[1:2, lanes] = delta
            spread.append((first, old * new, new, delta))
        for index in range(6):
            for place, head in enumerate(heads):
                lanes = lanes_of(head)
                first, old, new, delta = spread[place]
                if index < EARLY:
                    probs = early_weights[index + 1, :, lanes] * first
                    grad = early_grads[index + 1, :, lanes]
                elif index == EARLY:
                    probs, grad = mid_weights[:, lanes] * old, mid_grads[:, lanes]
                else:
                    probs = weights[place][index - EARLY - 1] * new
                    grad = grads[place][index - EARLY - 1]
                dscores = (probs * (grad - delta)).astype(jnp.bfloat16)
                probs = probs.astype(jnp.bfloat16)
                dscores_out[index, :, lanes] = dscores
                out = terms[index]
                out[KEYS, lanes] = dot(dscores, asks[KEYS, lanes], 1, 0).astype(out.dtype)
                out[VALUES, lanes] = dot(probs, asks[VALUES, lanes], 1, 0).astype(out.dtype)


def own_kernel(asks, early_weights, early_grads, final, dscores, own, *refs):
    blocks, parts, (query_out, own_out) = refs[:6], refs[6 : 6 + SUMMED], refs[6 + SUMMED :]
    for heads in GROUPS:
        span = [lanes_of(head) for head in heads]
        probs = [early_weights[0, :, l] * final[0:1, l] for l in span]
        mine = [
            (p * (early_grads[0, :, l] - final[1:2, l])).astype(jnp.bfloat16)
            for p, l in zip(probs, span)
        ]
        probs = [p.astype(jnp.bfloat16) for p in probs]
        grads = [dot(m, own[KEYS, l], 0, 0) for m, l in zip(mine, span)]
        for index in range(6):
            grads = [
                grad + dot(dscores[index, :, l], blocks[index][KEYS, l], 0, 0)
                for grad, l in zip(grads, span)
            ]
        for low, rows in ((mine, KEYS), (probs, VALUES)):
            totals = [dot(m, asks[rows, l], 1, 0) for m, l in zip(low, span)]
            for total, l in zip(totals, span):
                own_out[rows, l] = total + summed(
                    [part[rows, l].astype(jnp.float32) for part in parts]
                )
        for grad, l in zip(grads, span):
            query_out[:, l] = (grad * SCALE).astype(query_out.dtype)


def sum_kernel(own, *refs):
    parts, (key_out, value_out, held, sems) = refs[:-4], refs[-4:]
    copies = []
    for half, rows, out, scale in ((0, VALUES, value_out, 1.0), (1, KEYS, key_out, SCALE)):
        total = own[rows, :]
        for part in parts:
            total = total + part[rows, :].astype(jnp.float32)
        held[half] = (total * scale).astype(held.dtype)
        copies.append(pltpu.make_async_copy(held.at[half], out, sems.at[half]))
        copies[-1].start()
    for copy in copies:
        copy.wait()


FAR = pl.BlockSpec(memory_space=pltpu.HBM)
VM = pl.BlockSpec(memory_space=pltpu.VMEM)
SM = pl.BlockSpec(memory_space=pltpu.SMEM)
WIDE = (2 * BLOCK, HEADS * HD)
NARROW = (BLOCK, HEADS * HD)


NEAR = pltpu.VMEM
PLAIN = jax.ShapeDtypeStruct


def BLOCKED(shape, dtype):
    return PLAIN(shape, dtype)


def far(array):
    return pltpu.with_memory_space_constraint(array, pltpu.HBM)


def call(kernel, ins, outs, name, scratch=()):
    return pl.pallas_call(
        kernel,
        out_shape=[
            place(shape, dtype) for place, shape, dtype in outs
        ],
        in_specs=ins,
        out_specs=[FAR if place is PLAIN else VM for place, _, _ in outs],
        scratch_shapes=list(scratch),
        compiler_params=pltpu.CompilerParams(vmem_limit_bytes=40 * 1024 * 1024),
        name=name,
    )


def on_device(query, keys, values, dout, partners, counts):
    low, full = jnp.bfloat16, jnp.float32
    stats_row = (NEAR, (8, HEADS * HD), full)
    (own,) = call(
        pack_kernel, [FAR] * 2, [(NEAR, WIDE, low)], "pack", [pltpu.SemaphoreType.DMA((2,))]
    )(far(keys), far(values))
    asks, biases = call(
        load_kernel,
        [FAR] * 3,
        [(NEAR, WIDE, low), stats_row],
        "load",
        [pltpu.SMEM((1, 7), jnp.int32), pltpu.SemaphoreType.DMA((3,))],
    )(far(partners), far(query), far(dout))
    blocks = [swapped(own, index) for index in range(6)]
    weights, grads, stats = call(
        early_kernel,
        [VM] * (3 + EARLY),
        [(NEAR, (EARLY + 1,) + NARROW, full)] * 2 + [stats_row],
        "early",
    )(asks, biases, own, *blocks[:EARLY][::-1])
    mid_weights, mid_grads, mid_stats = call(
        middle_kernel, [VM] * 4, [(NEAR, NARROW, full)] * 2 + [stats_row], "middle"
    )(asks, biases, stats, blocks[EARLY])
    outs = call(
        late_kernel,
        [VM] * (8 + 5 - EARLY),
        [(NEAR, WIDE, low)] * 6 + [(NEAR, (6,) + NARROW, low), stats_row],
        "late",
    )(
        asks, biases, weights, grads, stats, mid_weights, mid_grads, mid_stats,
        *blocks[EARLY + 1 :][::-1],
    )
    terms, dscores, final = outs[:6], outs[6], outs[7]
    arrived = [swapped(terms[index], index) for index in BACK]
    query_out, own_out = call(
        own_kernel, [VM] * (12 + SUMMED), [(BLOCKED, NARROW, low), (NEAR, WIDE, full)], "own"
    )(asks, weights, grads, final, dscores, own, *blocks, *arrived[:SUMMED])
    key_out, value_out = call(sum_kernel, [VM] * (7 - SUMMED), [(PLAIN, NARROW, low)] * 2, "sums",
        [pltpu.VMEM((2,) + NARROW, low), pltpu.SemaphoreType.DMA((2,))],
    )(
        own_out, *arrived[SUMMED:]
    )
    return query_out, key_out, value_out


def solution(mesh):
    tokens = P(AXES, None)
    return jax.shard_map(
        on_device,
        mesh=mesh,
        in_specs=(tokens, tokens, tokens, tokens, tokens, P(AXES)),
        out_specs=(tokens, tokens, tokens),
        check_vma=False,
    )
```

```python
import functools

import jax
import jax.numpy as jnp
from jax import lax
from jax.experimental import pallas as pl
from jax.experimental.pallas import tpu as pltpu
from jax.sharding import PartitionSpec as P

HEADS = 6
HD = 128
BLOCK = 128
AXES = ("inner", "outer")
SCALE = HD ** -0.5
SCALE2 = SCALE * 1.4426950408889634
NEG = -1e30
STEP = {"x": 16, "y": 64, "z": 1}
SIZE = {"x": 4, "y": 8, "z": 16}
BLOCKS = 512
ROUTES = (
    (("z", 1), ("z", 1)),
    (("x", 0), ("y", 0)),
    (("x", 1), ("y", 1)),
    (("y", 0), ("x", 0)),
    (("y", 1), ("x", 1)),
    (("z", 0), ("z", 0)),
)
GROUPS = ((0, 1, 2, 3, 4, 5),)
EARLY = 4
BACK = (0, 1, 2, 3, 4, 5)
SUMMED = 3


def route_pairs(route):
    found = []
    for block in range(BLOCKS):
        name, odd = route[block & 1]
        place = (block // STEP[name]) % SIZE[name]
        sign = 1 - 2 * ((place + odd) & 1)
        if 0 <= place + sign < SIZE[name]:
            found.append((block, block + sign * STEP[name]))
    return found


def swapped(message, index):
    return lax.ppermute(message, AXES, route_pairs(ROUTES[index]))


def partner_of(me, index):
    targets = []
    for name, odd in ROUTES[index]:
        place = lax.div(me, jnp.int32(STEP[name])) & (SIZE[name] - 1)
        sign = 1 - 2 * ((place + odd) & 1)
        targets.append(me + sign * STEP[name])
    return jnp.where((me & 1) == 0, targets[0], targets[1])


def bias_of(partners, me, index):
    target = partner_of(me, index)
    listed = jnp.int32(0)
    for slot in range(1, 7):
        listed = listed | (partners[0, slot] == target).astype(jnp.int32)
    return jnp.where(listed > 0, jnp.float32(0.0), jnp.float32(NEG))


def dot(a, b, da, db):
    return lax.dot_general(a, b, (((da,), (db,)), ((), ())), preferred_element_type=jnp.float32)


KEYS = pl.ds(0, BLOCK)
VALUES = pl.ds(BLOCK, BLOCK)


def lanes_of(head):
    return pl.ds(head * HD, HD)


def summed(items):
    return functools.reduce(jnp.add, items)


def weigh(blocks, biases, asks, heads, before=None):
    span = [lanes_of(head) for head in heads]
    scores = [[dot(block[KEYS, l], asks[KEYS, l], 1, 1) for block in blocks] for l in span]
    grads = [[dot(block[VALUES, l], asks[VALUES, l], 1, 1) for block in blocks] for l in span]
    tops = [
        functools.reduce(
            jnp.maximum,
            [
                jnp.max(s, axis=0, keepdims=True) * SCALE2 + bias[:, l]
                for s, bias in zip(row, biases)
            ]
            + ([before[:, l]] if before is not None else []),
        )
        for row, l in zip(scores, span)
    ]
    weights = [
        [jnp.exp2(s * SCALE2 + (bias[:, l] - top)) for s, bias in zip(row, biases)]
        for row, top, l in zip(scores, tops, span)
    ]
    totals = [summed([jnp.sum(w, axis=0, keepdims=True) for w in row]) for row in weights]
    deltas = [
        summed([jnp.sum(w * g, axis=0, keepdims=True) for w, g in zip(row, more)])
        for row, more in zip(weights, grads)
    ]
    return weights, grads, tops, totals, deltas


def copied(pairs, sems):
    copies = [
        pltpu.make_async_copy(source, target, sems.at[i])
        for i, (source, target) in enumerate(pairs)
    ]
    for copy in copies:
        copy.start()
    return copies


def pack_kernel(keys, values, own, sems):
    for copy in copied(((keys, own.at[KEYS, :]), (values, own.at[VALUES, :])), sems):
        copy.wait()


def load_kernel(partners, query, dout, asks, bias_out, partner_list, sems):
    copies = copied(
        ((partners, partner_list), (query, asks.at[KEYS, :]), (dout, asks.at[VALUES, :])), sems
    )
    copies[0].wait()
    me = partner_list[0, 0]
    for index in range(6):
        bias = bias_of(partner_list, me, index)
        bias_out[index : index + 1, :] = jnp.full((1, HEADS * HD), bias, jnp.float32)
    for copy in copies[1:]:
        copy.wait()


def early_kernel(asks, biases, own, *refs):
    blocks, refs = (own,) + refs[:EARLY][::-1], refs[EARLY:]
    weights_out, grads_out, stats_out = refs
    rows = [jnp.zeros((1, HEADS * HD), jnp.float32)]
    rows += [biases[index : index + 1, :] for index in range(EARLY)]
    for heads in GROUPS:
        weights, grads, tops, totals, deltas = weigh(blocks, rows, asks, heads)
        for place, head in enumerate(heads):
            lanes = lanes_of(head)
            for index in range(EARLY + 1):
                weights_out[index, :, lanes] = weights[place][index]
                grads_out[index, :, lanes] = grads[place][index]
            stats_out[0:1, lanes] = tops[place]
            stats_out[1:2, lanes] = totals[place]
            stats_out[2:3, lanes] = deltas[place]


def late_kernel(asks, biases, early_weights, early_grads, stats, *refs):
    late = 6 - EARLY
    blocks, refs = refs[:late][::-1], refs[late:]
    terms, dscores_out, final_out = refs[:6], refs[6], refs[7]
    rows = [biases[index : index + 1, :] for index in range(EARLY, 6)]
    before = stats[0:1, :]
    for heads in GROUPS:
        weights, grads, tops, totals, deltas = weigh(blocks, rows, asks, heads, before)
        spread = []
        for place, head in enumerate(heads):
            lanes = lanes_of(head)
            old = jnp.exp2(before[:, lanes] - tops[place])
            new = 1.0 / (totals[place] + stats[1:2, lanes] * old)
            delta = (deltas[place] + stats[2:3, lanes] * old) * new
            final_out[0:1, lanes] = old * new
            final_out[1:2, lanes] = delta
            spread.append((old * new, new, delta))
        for index in range(6):
            for place, head in enumerate(heads):
                lanes = lanes_of(head)
                old, new, delta = spread[place]
                if index < EARLY:
                    probs = early_weights[index + 1, :, lanes] * old
                    grad = early_grads[index + 1, :, lanes]
                else:
                    probs = weights[place][index - EARLY] * new
                    grad = grads[place][index - EARLY]
                dscores = (probs * (grad - delta)).astype(jnp.bfloat16)
                probs = probs.astype(jnp.bfloat16)
                dscores_out[index, :, lanes] = dscores
                out = terms[index]
                out[KEYS, lanes] = dot(dscores, asks[KEYS, lanes], 1, 0).astype(out.dtype)
                out[VALUES, lanes] = dot(probs, asks[VALUES, lanes], 1, 0).astype(out.dtype)


def own_kernel(asks, early_weights, early_grads, final, dscores, own, *refs):
    blocks, parts, (query_out, own_out) = refs[:6], refs[6 : 6 + SUMMED], refs[6 + SUMMED :]
    for heads in GROUPS:
        span = [lanes_of(head) for head in heads]
        probs = [early_weights[0, :, l] * final[0:1, l] for l in span]
        mine = [
            (p * (early_grads[0, :, l] - final[1:2, l])).astype(jnp.bfloat16)
            for p, l in zip(probs, span)
        ]
        probs = [p.astype(jnp.bfloat16) for p in probs]
        grads = [dot(m, own[KEYS, l], 0, 0) for m, l in zip(mine, span)]
        for index in range(6):
            grads = [
                grad + dot(dscores[index, :, l], blocks[index][KEYS, l], 0, 0)
                for grad, l in zip(grads, span)
            ]
        for low, rows in ((mine, KEYS), (probs, VALUES)):
            totals = [dot(m, asks[rows, l], 1, 0) for m, l in zip(low, span)]
            for total, l in zip(totals, span):
                own_out[rows, l] = total + summed(
                    [part[rows, l].astype(jnp.float32) for part in parts]
                )
        for grad, l in zip(grads, span):
            query_out[:, l] = (grad * SCALE).astype(query_out.dtype)


def sum_kernel(own, *refs):
    parts, (key_out, value_out) = refs[:-2], refs[-2:]
    for rows, out, scale in ((KEYS, key_out, SCALE), (VALUES, value_out, 1.0)):
        total = own[rows, :]
        for part in parts:
            total = total + part[rows, :].astype(jnp.float32)
        out[...] = (total * scale).astype(out.dtype)


FAR = pl.BlockSpec(memory_space=pltpu.HBM)
VM = pl.BlockSpec(memory_space=pltpu.VMEM)
SM = pl.BlockSpec(memory_space=pltpu.SMEM)
WIDE = (2 * BLOCK, HEADS * HD)
NARROW = (BLOCK, HEADS * HD)


NEAR = pltpu.VMEM
PLAIN = jax.ShapeDtypeStruct


def far(array):
    return pltpu.with_memory_space_constraint(array, pltpu.HBM)


def call(kernel, ins, outs, name, scratch=()):
    return pl.pallas_call(
        kernel,
        out_shape=[
            place(shape, dtype) for place, shape, dtype in outs
        ],
        in_specs=ins,
        out_specs=[VM] * len(outs),
        scratch_shapes=list(scratch),
        compiler_params=pltpu.CompilerParams(vmem_limit_bytes=40 * 1024 * 1024),
        name=name,
    )


def on_device(query, keys, values, dout, partners, counts):
    low, full = jnp.bfloat16, jnp.float32
    stats_row = (NEAR, (8, HEADS * HD), full)
    (own,) = call(
        pack_kernel, [FAR] * 2, [(NEAR, WIDE, low)], "pack", [pltpu.SemaphoreType.DMA((2,))]
    )(far(keys), far(values))
    asks, biases = call(
        load_kernel,
        [FAR] * 3,
        [(NEAR, WIDE, low), stats_row],
        "load",
        [pltpu.SMEM((1, 7), jnp.int32), pltpu.SemaphoreType.DMA((3,))],
    )(far(partners), far(query), far(dout))
    blocks = [swapped(own, index) for index in range(6)]
    weights, grads, stats = call(
        early_kernel,
        [VM] * (3 + EARLY),
        [(NEAR, (EARLY + 1,) + NARROW, full)] * 2 + [stats_row],
        "early",
    )(asks, biases, own, *blocks[:EARLY][::-1])
    outs = call(
        late_kernel,
        [VM] * (5 + 6 - EARLY),
        [(NEAR, WIDE, low)] * 6 + [(NEAR, (6,) + NARROW, low), stats_row],
        "late",
    )(asks, biases, weights, grads, stats, *blocks[EARLY:][::-1])
    terms, dscores, final = outs[:6], outs[6], outs[7]
    arrived = [swapped(terms[index], index) for index in BACK]
    query_out, own_out = call(
        own_kernel, [VM] * (12 + SUMMED), [(PLAIN, NARROW, low), (NEAR, WIDE, full)], "own"
    )(asks, weights, grads, final, dscores, own, *blocks, *arrived[:SUMMED])
    key_out, value_out = call(sum_kernel, [VM] * (7 - SUMMED), [(PLAIN, NARROW, low)] * 2, "sums")(
        own_out, *arrived[SUMMED:]
    )
    return query_out, key_out, value_out


def solution(mesh):
    tokens = P(AXES, None)
    return jax.shard_map(
        on_device,
        mesh=mesh,
        in_specs=(tokens, tokens, tokens, tokens, tokens, P(AXES)),
        out_specs=(tokens, tokens, tokens),
        check_vma=False,
    )
```
